128 devices in a mesh: row: 8 (over z, core), col: 16 (over y, x).
Axes of the slice: x: 4, y: 4, z: 4, core: 2. Of those that a mesh axis runs over, the one named last changes fastest.
Arguments:
- noise: float32 [4096, 2048], P(('row', 'col')), may hold values from -22 to 22
- data: float32 [16384, 2048], P(('col', 'row')), may hold values from -22 to 22
- times: float32 [4096], P(('row', 'col')), may hold values from 0 to 1
Outputs:
- path: float32 [4096, 2048], P(('row', 'col'))
- velocity: float32 [4096, 2048], P(('row', 'col'))
The draws below stay inside these ranges and needn't reach their ends.
All inputs are finite; a program needn't handle non-finite values.
Results may differ from the reference program's by a relative error of at most 0.0003.
Values sent between devices are 32-bit elements; how exact they have to be, the bound alone decides.
No kernel may reach another device: no remote copies, remote signals or barrier semaphores. Data moves between devices by JAX's collectives and lax.ppermute only.
A program may use at most 192 MiB of HBM per device.

```python
import math
import jax
import jax.numpy as jnp
from jax import lax

D = 2048
DATA_BLK = 1024
ITERS = 2
NOISE = 4096
DATA = 16384


def cluster_means(key):
    groups = DATA // DATA_BLK
    means = jnp.clip(jax.random.normal(jax.random.fold_in(key, 7), (groups, D), jnp.float32), -3.0, 3.0)
    return means * 0.3


def scaled_codes(key, columns):
    first_key = jax.random.fold_in(key, 0)
    base = jnp.clip(jax.random.normal(first_key, (columns, D), jnp.float32), -5.5, 5.5)
    return base


def data_codes(key):
    means = cluster_means(key)
    labels = jnp.arange(DATA, dtype=jnp.int32) // DATA_BLK
    picked = jnp.take(means, labels, axis=0)
    return scaled_codes(jax.random.fold_in(key, 23), DATA) + picked


def draw_noise(key, part):
    means = cluster_means(key)
    key = jax.random.fold_in(key, 11)
    groups = DATA // DATA_BLK
    labels = jnp.arange(NOISE, dtype=jnp.int32) % groups
    picked = jnp.take(means, labels, axis=0)
    return (scaled_codes(key, NOISE) + picked).astype(jnp.float32)


def draw_data(key, part):
    return data_codes(key).astype(jnp.float32)


def block_levels(stream_key, shape, shards, least, top_value):
    gain = 1.0
    for axis_at, shards_of in shards:
        draws = jax.random.uniform(jax.random.fold_in(jax.random.fold_in(stream_key, 6), axis_at), (shards_of,), jnp.float32, least / len(shards), top_value / len(shards))
        gain = gain * jnp.repeat(jnp.exp(draws), shape[axis_at] // shards_of).reshape((-1,) + (1,) * (len(shape) - 1 - axis_at))
    return gain


def setup_inputs(seed: int = 0) -> dict:
    splits = jax.random.split(jax.random.key(seed), 4)
    return {
        "noise": draw_noise(jax.random.fold_in(splits[3], 71), 0),
        "data": draw_data(jax.random.fold_in(splits[3], 71), 0),
        "times": jnp.clip(1.0 * jax.random.uniform(splits[2], (NOISE,), jnp.float32) ** block_levels(splits[2], (NOISE,), ((0, 128),), -0.2, 0.2), 0.0, 1.0),
    }


epsilon = 0.05
highest = lax.Precision.HIGHEST


def cost_block(rows, row_norms, cols, col_norms):
    cross = lax.dot_general(rows, cols, (((1,), (1,)), ((), ())), precision=highest)
    return (row_norms[:, None] + col_norms[None, :] - 2.0 * cross) / D


def reference(noise, data, times):
    row_norms = jnp.sum(noise * noise, axis=1)
    col_norms = jnp.sum(data * data, axis=1)
    block_rows = min(512, NOISE)
    block_count = NOISE // block_rows
    row_blocks = noise.reshape(block_count, block_rows, D)
    norm_blocks = row_norms.reshape(block_count, block_rows)
    col_pot = jnp.zeros((DATA,), jnp.float32)
    for step in range(ITERS):
        def row_lse(args):
            scores = (col_pot[None, :] - cost_block(args[0], args[1], data, col_norms)) / epsilon
            peak = jnp.max(scores, axis=1)
            return peak + jnp.log(jnp.sum(jnp.exp(scores - peak[:, None]), axis=1))

        lse_rows = lax.map(row_lse, (row_blocks, norm_blocks)).reshape(NOISE)
        row_pot = epsilon * math.log(DATA) - epsilon * lse_rows
        pot_blocks = row_pot.reshape(block_count, block_rows)

        def col_step(carry, args):
            scores = (args[2][:, None] - cost_block(args[0], args[1], data, col_norms)) / epsilon
            peak = jnp.maximum(carry[0], jnp.max(scores, axis=0))
            total = carry[1] * jnp.exp(carry[0] - peak) + jnp.sum(jnp.exp(scores - peak[None, :]), axis=0)
            return (peak, total), None

        start = (jnp.full((DATA,), -jnp.inf, jnp.float32), jnp.zeros((DATA,), jnp.float32))
        (peaks, totals), _ = lax.scan(col_step, start, (row_blocks, norm_blocks, pot_blocks))
        col_pot = epsilon * math.log(NOISE) - epsilon * (peaks + jnp.log(totals))

    def target_block(args):
        scores = (col_pot[None, :] - cost_block(args[0], args[1], data, col_norms)) / epsilon
        peak = jnp.max(scores, axis=1)
        weights = jnp.exp(scores - peak[:, None])
        denom = jnp.sum(weights, axis=1)
        numer = jnp.dot(weights, data, precision=highest)
        return numer / denom[:, None]

    targets = lax.map(target_block, (row_blocks, norm_blocks)).reshape(NOISE, D)
    path = (1.0 - times)[:, None] * noise + times[:, None] * targets
    velocity = targets - noise
    return path, velocity
```

```python
import math

import jax
import jax.numpy as jnp
from jax import lax
from jax.sharding import PartitionSpec as P

EPS = 0.05
BOTH = ("row", "col")


def swap_col(value, masks):
    pairs = [
        (row * 16 + col, row * 16 + (col ^ masks[row % 2])) for row in range(8) for col in range(16)
    ]
    return lax.ppermute(value, BOTH, pairs)


def swap_z(value, masks):
    pairs = [
        (row * 16 + col, (row ^ (2 * masks[row % 2])) * 16 + col)
        for row in range(8)
        for col in range(16)
    ]
    return lax.ppermute(value, BOTH, pairs)


def swap_core(value):
    return lax.ppermute(value, "row", [(row, row ^ 1) for row in range(8)])


XA, XB, YA, YB = (1, 3), (3, 1), (4, 12), (12, 4)
ZA, ZB = (1, 3), (3, 1)
HIGH = lax.Precision.HIGH


def join(parts, axis=0):
    return jnp.concatenate(parts, axis=axis)


def gather_noise(part, steps):
    for masks in steps:
        part = join([part, swap_col(part, masks)])
    return part


def turn(rows):
    width = rows.shape[1:]
    return rows.reshape((4, 4, 32) + width).swapaxes(0, 1).reshape((512,) + width)


def row_exchange(value, combine):
    keep = value.shape[0]
    for bit, masks in enumerate((XA, XB, YA, YB)):
        other = swap_col(value, masks)
        other = other.reshape(keep, 2 ** (3 - bit), 2, 2**bit * 32)
        other = other[:, :, ::-1].reshape(keep, 512)
        value = combine(value, other)
    return value


def col_exchange(value, combine):
    orders = ([1, 0, 3, 2, 6, 7, 4, 5], [2, 3, 0, 1, 5, 4, 7, 6], [4, 5, 6, 7, 0, 1, 2, 3])
    swaps = (lambda v: swap_z(v, ZA), lambda v: swap_z(v, ZB), swap_core)
    for order, swap in zip(orders, swaps):
        other = swap(value)
        other = join([other[:, i : i + 1] for i in order], axis=1)
        value = combine(value, other)
    return value


def join_lse(one, two):
    peak = jnp.maximum(one[0], two[0])
    total = one[1] * jnp.exp(one[0] - peak) + two[1] * jnp.exp(two[0] - peak)
    return jnp.stack([peak, total])


def add(one, two):
    return one + two


def scatter_sum(half, steps):
    for masks in steps:
        rows = half.shape[0] // 2
        half = half[:rows] + swap_col(half[rows:], masks)
    return half


def per_device(noise, data, times):
    features = noise.shape[1]
    middle = features // 2
    noise_count, data_count = 4096, 16384
    scale = 1.0 / (features * EPS)

    own = [data, swap_z(data, ZA), swap_z(data, ZB)]
    own.append(swap_z(own[1], ZB))
    cols = [join([piece, swap_core(piece)]) for piece in own]

    first = gather_noise(noise[:, :middle], (XA, XB, YA, YB))
    second = turn(gather_noise(noise[:, middle:], (YA, YB, XA, XB)))
    rows = join([first, second], axis=1)
    row_sq = jnp.sum(rows * rows, axis=1)

    blocks = []
    for piece in cols:
        col_sq = jnp.sum(piece * piece, axis=1)
        cross = lax.dot_general(rows, piece, (((1,), (1,)), ((), ())), precision=HIGH)
        blocks.append((2.0 * cross - row_sq[:, None] - col_sq[None, :]) * scale)
    score = join([block[:, :128] for block in blocks] + [block[:, 128:] for block in blocks], 1)
    order_cols = join([piece[:128] for piece in cols] + [piece[128:] for piece in cols])

    peak = jnp.max(score, axis=1)
    total = jnp.sum(jnp.exp(score - peak[:, None]), axis=1)
    peak, total = row_exchange(jnp.stack([peak, total]), join_lse)
    row_pot = math.log(data_count) - (peak + jnp.log(total))

    shifted = score + row_pot[:, None]
    low = jnp.max(shifted, axis=0)
    plan = jnp.exp(shifted - low[None, :])
    total = jnp.sum(plan, axis=0)
    top, total = col_exchange(jnp.stack([low, total]).reshape(2, 8, 128), join_lse)
    gain = noise_count * jnp.exp(low - top.reshape(-1)) / total.reshape(-1)

    totals = jnp.sum(plan * gain[None, :], axis=1)
    totals = row_exchange(totals[None], add)[0]
    scale_rows = data_count / totals
    totals = jnp.sum(plan * scale_rows[:, None], axis=0) * gain
    totals = col_exchange(totals.reshape(1, 8, 128), add).reshape(-1)
    gain = gain * (noise_count / totals)

    weights = plan * gain[None, :]
    denom = scatter_sum(jnp.sum(weights, axis=1)[:, None], (YB, YA, XB, XA))
    left = scatter_sum(
        jnp.dot(weights, order_cols[:, :middle], precision=HIGH), (YB, YA, XB, XA)
    )
    right = scatter_sum(
        jnp.dot(turn(weights), order_cols[:, middle:], precision=HIGH), (XB, XA, YB, YA)
    )
    targets = join([left, right], axis=1) / denom
    path = (1.0 - times)[:, None] * noise + times[:, None] * targets
    velocity = targets - noise
    return path, velocity


def solution(mesh):
    in_specs = (P(("row", "col"), None), P(("col", "row"), None), P(("row", "col")))
    out_specs = (P(("row", "col"), None), P(("row", "col"), None))
    return jax.shard_map(
        per_device, mesh=mesh, in_specs=in_specs, out_specs=out_specs, check_vma=False
    )
```

```python
import math

import jax
import jax.numpy as jnp
from jax import lax
from jax.experimental import pallas as pl
from jax.experimental.pallas import tpu as pltpu
from jax.sharding import PartitionSpec as P

EPS = 0.05
LIMIT = 14
BOTH = ("row", "col")
NOISE, DATA = 4096, 16384
ROWS, COLS = 512, 1024
BF, F32 = jnp.bfloat16, jnp.float32

XA, XB, YA, YB = (1, 3), (3, 1), (4, 12), (12, 4)
ZA, ZB = (1, 3), (3, 1)


def swap_col(value, masks):
    pairs = [
        (row * 16 + col, row * 16 + (col ^ masks[row % 2])) for row in range(8) for col in range(16)
    ]
    return lax.ppermute(value, BOTH, pairs)


def swap_z(value, masks):
    pairs = [
        (row * 16 + col, (row ^ (2 * masks[row % 2])) * 16 + col)
        for row in range(8)
        for col in range(16)
    ]
    return lax.ppermute(value, BOTH, pairs)


def swap_core(value):
    return lax.ppermute(value, "row", [(row, row ^ 1) for row in range(8)])


def row_places():
    tables = []
    for core in range(2):
        masks = [m[core] for m in (XA, XB, YA, YB)]
        table = []
        for p in range(16):
            rel = 0
            for bit in range(4):
                rel ^= masks[bit] if p >> bit & 1 else 0
            table.append(rel)
        tables.append(table)
    core = lax.axis_index("row") % 2
    table = jnp.where(core == 0, jnp.array(tables[0], jnp.int32), jnp.array(tables[1], jnp.int32))
    return table ^ lax.axis_index("col").astype(jnp.int32)


def col_places():
    tables = []
    for core in range(2):
        table = []
        for k in range(4):
            for sibling in range(2):
                of = core ^ sibling
                z = (ZA[of] if k & 1 else 0) ^ (ZB[of] if k & 2 else 0)
                table.append(z * 2 + sibling)
        tables.append(table + [0])
    row = lax.axis_index("row").astype(jnp.int32)
    table = jnp.where(row % 2 == 0, jnp.array(tables[0], jnp.int32), jnp.array(tables[1], jnp.int32))
    return table ^ row


def vmem(count):
    return [pl.BlockSpec(memory_space=pltpu.VMEM)] * count


def smem(count):
    return [pl.BlockSpec(memory_space=pltpu.SMEM)] * count


def call(body, outs, places=0, arrays=0, scratch=(), flops=0, moved=0, limit=LIMIT, far=0, far_out=0):
    out_specs = jax.tree.map(lambda _: pl.BlockSpec(memory_space=pltpu.VMEM), outs)
    if far_out:
        out_specs = out_specs[:-far_out] + (pl.BlockSpec(memory_space=pltpu.HBM),) * far_out
    return pl.pallas_call(
        body,
        out_shape=outs,
        in_specs=smem(places) + [pl.BlockSpec(memory_space=pltpu.HBM)] * far + vmem(arrays),
        out_specs=out_specs,
        scratch_shapes=list(scratch),
        compiler_params=pltpu.CompilerParams(vmem_limit_bytes=limit * 2**20),
        cost_estimate=pl.CostEstimate(flops=flops, bytes_accessed=moved, transcendentals=0),
    )


def shape(dims, dtype=F32):
    return jax.ShapeDtypeStruct(dims, dtype)


def split(value):
    high = value.astype(BF)
    return high, (value - high.astype(F32)).astype(BF)


def diagonal():
    one = lax.broadcasted_iota(jnp.int32, (128, 128), 0)
    return one == lax.broadcasted_iota(jnp.int32, (128, 128), 1)


def compact(ref):
    eye = diagonal()
    return jnp.concatenate(
        [
            jnp.sum(jnp.where(eye, ref[128 * q : 128 * q + 128, :], 0.0), axis=0, keepdims=True)
            for q in range(4)
        ],
        axis=0,
    )


def spread(value, ref):
    eye = diagonal()
    for q in range(4):
        wide = jnp.broadcast_to(value[q : q + 1, :], (128, 128))
        column = jnp.sum(jnp.where(eye, wide, 0.0), axis=1, keepdims=True)
        ref[128 * q : 128 * q + 128, :] = jnp.broadcast_to(column, (128, 128))


def block(p):
    return pl.ds(32 * p, 32)


def place(places, p):
    return pl.ds(pl.multiple_of(places[p] * 32, 32), 32)


def dot_t(one, two):
    return lax.dot_general(one, two, (((1,), (1,)), ((), ())), preferred_element_type=F32)


def group(k, pieces, high, low, norm):
    for at, ref in ((0, pieces[2 * k]), (128, pieces[2 * k + 1])):
        for p in range(4):
            rows = slice(256 * k + at + 32 * p, 256 * k + at + 32 * p + 32)
            value = ref[32 * p : 32 * p + 32, :]
            high[rows, :], low[rows, :] = split(value)
            total = jnp.sum(value * value, axis=1, keepdims=True)
            norm[at + 32 * p : at + 32 * p + 32, :] = jnp.broadcast_to(total, (32, 128))


def score(k, scale, terms, nn, high, low, norm, out, lanes):
    eye = diagonal()
    norms = jnp.concatenate(
        [
            jnp.sum(jnp.where(eye, norm[128 * q : 128 * q + 128, :], 0.0), axis=0, keepdims=True)
            for q in range(2)
        ],
        axis=1,
    )
    cols = slice(256 * k, 256 * k + 256)
    both = dot_t(terms[...], high[cols, :])
    cross = both[:ROWS] + both[ROWS:] + dot_t(terms[:ROWS, :], low[cols, :])
    out[:, lanes] = (2.0 * cross - nn[:, :1] - norms) * scale


def data_body(*refs):
    pieces, norms, (dh, dl), (high, low, outs) = refs[:6], refs[6], refs[7:9], refs[9:]
    sent = []
    for k in range(3):
        group(k, pieces, high, low, norms.at[256 * k : 256 * k + 256, :])
        rows = slice(256 * k, 256 * k + 256)
        for i, (source, target) in enumerate(((high, dh), (low, dl))):
            sent.append(
                pltpu.make_async_copy(source.at[rows, :], target.at[rows, :], outs.at[2 * k + i])
            )
            sent[-1].start()
    for copy in sent:
        copy.wait()


def row_sums(value):
    peak = jnp.max(value, axis=1, keepdims=True)
    total = jnp.sum(jnp.exp(value - peak), axis=1, keepdims=True)
    return jnp.broadcast_to(peak, (32, 128)), jnp.broadcast_to(total, (32, 128))


def early_body(scale, *refs):
    data, norms, noise = refs[0:2], refs[2], refs[3:7]
    terms, nn, scores, peaks, totals = refs[7:12]
    high, low, sems = refs[12:]
    copies = []
    for k in range(3):
        rows = slice(256 * k, 256 * k + 256)
        for i, (source, target) in enumerate(zip(data, (high, low))):
            copies.append(
                pltpu.make_async_copy(source.at[rows, :], target.at[rows, :], sems.at[2 * k + i])
            )
            copies[-1].start()
    middle = noise[0].shape[1]
    for p in range(16):
        xs, ys = p % 4, p // 4
        q = xs * 4 + ys
        one = noise[p // 8][32 * (p % 8) : 32 * (p % 8) + 32, :]
        two = noise[2 + q // 8][32 * (q % 8) : 32 * (q % 8) + 32, :]
        top, under = slice(32 * p, 32 * p + 32), slice(ROWS + 32 * p, ROWS + 32 * p + 32)
        terms[top, :middle], terms[under, :middle] = split(one)
        terms[top, middle:], terms[under, middle:] = split(two)
        total = jnp.sum(one * one + two * two, axis=1, keepdims=True)
        nn[32 * p : 32 * p + 32, :] = jnp.broadcast_to(total, (32, 128))
    for copy in copies:
        copy.wait()
    for k in range(3):
        rows = slice(256 * k, 256 * k + 256)
        score(k, scale, terms, nn, high, low, norms.at[rows, :], scores, rows)
    for p in range(16):
        peaks[block(p), :], totals[block(p), :] = row_sums(scores[block(p), :])


def late_body(scale, places, own, sibling, terms, nn, peaks, totals, scores, out, dh, dl, *scratch):
    high, low, norm, ends, sums, sems = scratch
    group(0, (own, sibling), high, low, norm)
    sent = [
        pltpu.make_async_copy(source, target, sems.at[i])
        for i, (source, target) in enumerate(((high, dh), (low, dl)))
    ]
    for copy in sent:
        copy.start()
    score(0, scale, terms, nn, high, low, norm, scores, slice(0, 256))
    for p in range(16):
        peak, total = row_sums(scores[block(p), :])
        before = peaks[block(p), :]
        top = jnp.maximum(peak, before)
        ends[place(places, p), :] = top
        sums[place(places, p), :] = total * jnp.exp(peak - top) + totals[block(p), :] * jnp.exp(
            before - top
        )
    value = jnp.concatenate([compact(ends), compact(sums)], axis=0)
    for to in range(16):
        out[to] = value
    for copy in sent:
        copy.wait()


def col_first_body(rplaces, cplaces, got, early, late, plan, out, pots, ends):
    peak = got[0, 0:4, :]
    for one in range(1, 16):
        peak = jnp.maximum(peak, got[one, 0:4, :])
    total = got[0, 4:8, :] * jnp.exp(got[0, 0:4, :] - peak)
    for one in range(1, 16):
        total = total + got[one, 4:8, :] * jnp.exp(got[one, 0:4, :] - peak)
    spread(math.log(DATA) - (peak + jnp.log(total)), pots)
    for k in range(4):
        lanes = slice(256 * k, 256 * k + 256)
        high = None
        for p in range(16):
            value = late[block(p), :] if k == 3 else early[block(p), lanes]
            value = value + pots[place(rplaces, p), :][:, :1]
            plan[block(p), lanes] = value
            value = jnp.max(value.reshape(4, 8, 256), axis=0)
            high = value if high is None else jnp.maximum(high, value)
        high = jnp.max(high, axis=0, keepdims=True)
        sums = None
        for p in range(16):
            value = jnp.exp(plan[block(p), lanes] - high)
            plan[block(p), lanes] = value
            value = jnp.sum(value.reshape(4, 8, 256), axis=0)
            sums = value if sums is None else sums + value
        sums = jnp.sum(sums, axis=0, keepdims=True)
        for half in range(2):
            at = cplaces[2 * k + half]
            ends[pl.ds(at, 1), :] = high[:, 128 * half : 128 * half + 128]
            ends[pl.ds(8 + at, 1), :] = sums[:, 128 * half : 128 * half + 128]
    for to in range(8):
        out[to] = ends[...]


def to_lanes(cplaces, ref):
    return jnp.concatenate([ref[pl.ds(cplaces[b], 1), :] for b in range(8)], axis=1)


def row_second_body(rplaces, cplaces, got, plan, out, gains, totals):
    high = got[0, 0:8, :]
    for one in range(1, 8):
        high = jnp.maximum(high, got[one, 0:8, :])
    total = got[0, 8:16, :] * jnp.exp(got[0, 0:8, :] - high)
    for one in range(1, 8):
        total = total + got[one, 8:16, :] * jnp.exp(got[one, 0:8, :] - high)
    own = got[pl.ds(cplaces[8], 1)][0, 0:8, :]
    gains[...] = NOISE * jnp.exp(own - high) / total
    lanes = to_lanes(cplaces, gains)
    for p in range(16):
        value = jnp.sum(plan[block(p), :] * lanes, axis=1, keepdims=True)
        totals[place(rplaces, p), :] = jnp.broadcast_to(value, (32, 128))
    value = compact(totals)
    value = jnp.concatenate([value, value], axis=0)
    for to in range(16):
        out[to] = value


def col_second_body(rplaces, cplaces, got, gains, plan, out, scales, ends):
    total = got[0, 0:4, :]
    for one in range(1, 16):
        total = total + got[one, 0:4, :]
    spread(DATA / total, scales)
    sums = None
    for p in range(16):
        value = plan[block(p), :] * scales[place(rplaces, p), :][:, :1]
        value = jnp.sum(value.reshape(4, 8, COLS), axis=0)
        sums = value if sums is None else sums + value
    sums = jnp.sum(sums, axis=0, keepdims=True)
    for b in range(8):
        ends[pl.ds(cplaces[b], 1), :] = sums[:, 128 * b : 128 * b + 128]
    value = ends[...] * gains[...]
    for to in range(8):
        out[to] = value


def weight_body(cplaces, got, gains, plan, high, low, denom, ends, totals):
    total = got[0]
    for one in range(1, 8):
        total = total + got[one]
    ends[...] = gains[...] * (NOISE / total)
    lanes = to_lanes(cplaces, ends)
    for p in range(16):
        value = plan[block(p), :] * lanes
        high[block(p), :], low[block(p), :] = split(value)
        totals[block(p), :] = jnp.broadcast_to(jnp.sum(value, axis=1, keepdims=True), (32, 128))
    denom[...] = totals[...]


def dot(one, two):
    return jnp.dot(one, two, preferred_element_type=F32)


def product_body(blocks, lanes, wh, wl, denom, h0, l0, h1, l1, out):
    terms = [
        jnp.concatenate([ref[block(p), at] for ref in (wh, wl) for p in blocks], axis=0)
        for at in (slice(0, 768), slice(768, 1024))
    ]
    for n in range(4):
        at = slice(lanes + 256 * n, lanes + 256 * n + 256)
        both = dot(terms[0], h0[:, at]) + dot(terms[1], h1[:, at])
        more = dot(terms[0][:256], l0[:, at]) + dot(terms[1][:256], l1[:, at])
        total = both[:256] + both[256:] + more
        for i in range(8):
            for t in range(2):
                tile = total[32 * i : 32 * i + 32, 128 * t : 128 * t + 128]
                out[i, 32 * (2 * n + t) : 32 * (2 * n + t) + 32, :] = tile
    if lanes == 0:
        eye = diagonal()[:32, :]
        for i, p in enumerate(blocks):
            row = jnp.sum(jnp.where(eye, denom[block(p), :], 0.0), axis=0, keepdims=True)
            out[i, 256:264, :] = jnp.broadcast_to(row, (8, 128))


def end_body(left, right, noise, times, path, velocity):
    eye = diagonal()[:32, :]
    wide = jnp.broadcast_to(left[0, 256:257, :], (32, 128))
    inverse = 1.0 / jnp.sum(jnp.where(eye, wide, 0.0), axis=1, keepdims=True)
    for side, ref in enumerate((left, right)):
        for t in range(8):
            lanes = slice(1024 * side + 128 * t, 1024 * side + 128 * t + 128)
            target = ref[0, 32 * t : 32 * t + 32, :] * inverse
            own = noise[:, lanes]
            at = times[:, :1]
            path[:, lanes] = (1.0 - at) * own + at * target
            velocity[:, lanes] = target - own


def after(*values):
    return lax.optimization_barrier(values)


def product(blocks, lanes, *arrays):
    def body(*refs):
        product_body(blocks, lanes, *refs)

    return call(
        body,
        shape((8, 264 if lanes == 0 else 256, 128)),
        0,
        7,
        flops=3 * 2 * 256 * 1024 * 1024,
        moved=6 * 2**20,
    )(*arrays)


X_FIRST = list(range(16))
Y_FIRST = [ys * 4 + xs for xs in range(4) for ys in range(4)]


def per_device(noise, data, times):
    features = noise.shape[1]
    middle = features // 2
    scale = 1.0 / (features * EPS)
    rplaces, cplaces = row_places(), col_places()

    near, far = swap_z(data, ZA), swap_z(data, ZB)
    parts = [noise[:, :middle], noise[:, middle:]]
    orders = ((XA, XB, YA, YB), (YA, YB, XA, XB))
    stages = []
    for step in range(3):
        parts = [
            jnp.concatenate([part, swap_col(part, order[step])], axis=0)
            for part, order in zip(parts, orders)
        ]
        stages.append(parts)
    last = [swap_col(part, order[3]) for part, order in zip(parts, orders)]
    first = data
    near = after(near, *stages[1])[0]
    own = [data, near, far, swap_z(near, ZB)]
    cross = [swap_core(first), swap_core(near), swap_core(far), swap_core(own[3])]
    pieces = [[part, one] for part, one in zip(parts, last)]

    wide = pltpu.VMEM((ROWS, 128), F32)
    norms, h0, l0 = call(
        data_body,
        (shape((768, 128)),) + (shape((768, features), BF),) * 2,
        arrays=6,
        scratch=(
            pltpu.VMEM((768, features), BF),
            pltpu.VMEM((768, features), BF),
            pltpu.SemaphoreType.DMA((6,)),
        ),
        moved=12 * 2**20,
        far_out=2,
    )(own[0], cross[0], own[1], cross[1], own[2], cross[2])
    rows, row_norms, early, peaks, totals = call(
        lambda *refs: early_body(scale, *refs),
        (shape((2 * ROWS, features), BF), shape((ROWS, 128)), shape((ROWS, 768)))
        + (shape((ROWS, 128)),) * 2,
        arrays=5,
        scratch=(
            pltpu.VMEM((768, features), BF),
            pltpu.VMEM((768, features), BF),
            pltpu.SemaphoreType.DMA((6,)),
        ),
        flops=3 * 2 * ROWS * 768 * features,
        moved=16 * 2**20,
        limit=20,
        far=2,
    )(h0, l0, norms, *pieces[0], *pieces[1])
    late, send, h1, l1 = call(
        lambda *refs: late_body(scale, *refs),
        (shape((ROWS, 256)), shape((16, 8, 128))) + (shape((256, features), BF),) * 2,
        1,
        6,
        scratch=(
            pltpu.VMEM((256, features), BF),
            pltpu.VMEM((256, features), BF),
            pltpu.VMEM((256, 128), F32),
            wide,
            wide,
            pltpu.SemaphoreType.DMA((2,)),
        ),
        flops=3 * 2 * ROWS * 256 * features,
        moved=8 * 2**20,
        far_out=2,
    )(rplaces, own[3], cross[3], rows, row_norms, peaks, totals)
    send, rplaces, cplaces = after(send, rplaces, cplaces)
    got = lax.all_to_all(send, "col", 0, 0)
    plan, send = call(
        col_first_body,
        (shape((ROWS, COLS)), shape((8, 16, 128))),
        2,
        3,
        (wide, pltpu.VMEM((16, 128), F32)),
    )(rplaces, cplaces, got, early, late)
    got = lax.all_to_all(send, "row", 0, 0)
    send, gains = call(
        row_second_body,
        (shape((16, 8, 128)), shape((8, 128))),
        2,
        2,
        (wide,),
    )(rplaces, cplaces, got, plan)
    got = lax.all_to_all(send, "col", 0, 0)
    send = call(
        col_second_body,
        shape((8, 8, 128)),
        2,
        3,
        (wide, pltpu.VMEM((8, 128), F32)),
    )(rplaces, cplaces, got, gains, plan)
    got = lax.all_to_all(send, "row", 0, 0)
    wh, wl, denom = call(
        weight_body,
        (shape((ROWS, COLS), BF), shape((ROWS, COLS), BF), shape((ROWS, 128))),
        1,
        3,
        (pltpu.VMEM((8, 128), F32), wide),
    )(cplaces, got, gains, plan)

    rest = (wh, wl, denom, h0, l0, h1, l1)
    left_out = product(X_FIRST[8:], 0, *rest)
    rest = after(left_out, *rest)
    left_out, rest = rest[0], rest[1:]
    right_out = product(Y_FIRST[8:], middle, *rest)
    rest = after(right_out, *rest)
    right_out, rest = rest[0], rest[1:]
    left_in, right_in = swap_col(left_out, YB), swap_col(right_out, XB)
    left = product(X_FIRST[:8], 0, *rest)
    rest = after(left, *rest)
    left, rest = rest[0], rest[1:]
    right = product(Y_FIRST[:8], middle, *rest)
    left, right = left + left_in, right + right_in
    for first, second in zip((YA, XB, XA), (XA, YB, YA)):
        rows = left.shape[0] // 2
        left_in, right_in = swap_col(left[rows:], first), swap_col(right[rows:], second)
        left, right = left[:rows] + left_in, right[:rows] + right_in
    wide_times = jnp.broadcast_to(times[:, None], (times.shape[0], 128))
    outs = (shape(noise.shape), shape(noise.shape))
    return call(end_body, outs, 0, 4)(left, right, noise, wide_times)


def solution(mesh):
    in_specs = (P(("row", "col"), None), P(("col", "row"), None), P(("row", "col")))
    out_specs = (P(("row", "col"), None), P(("row", "col"), None))
    return jax.shard_map(
        per_device, mesh=mesh, in_specs=in_specs, out_specs=out_specs, check_vma=False
    )
```

```python
import math

import jax
import jax.numpy as jnp
from jax import lax
from jax.experimental import pallas as pl
from jax.experimental.pallas import tpu as pltpu
from jax.sharding import PartitionSpec as P

EPS = 0.05
LIMIT = 14
BOTH = ("row", "col")
NOISE, DATA = 4096, 16384
ROWS, COLS = 512, 1024
BF, F32 = jnp.bfloat16, jnp.float32

UA, UB, VA, VB = (1, 4), (3, 12), (4, 1), (12, 3)
FIRST, SECOND = (VA, VB, UA, UB), (VB, VA, UB, UA)
ZA, ZB = (1, 3), (3, 1)


def swap_col(value, masks):
    pairs = [
        (row * 16 + col, row * 16 + (col ^ masks[row % 2])) for row in range(8) for col in range(16)
    ]
    return lax.ppermute(value, BOTH, pairs)


def swap_z(value, masks):
    pairs = [
        (row * 16 + col, (row ^ (2 * masks[row % 2])) * 16 + col)
        for row in range(8)
        for col in range(16)
    ]
    return lax.ppermute(value, BOTH, pairs)


def swap_core(value):
    return lax.ppermute(value, "row", [(row, row ^ 1) for row in range(8)])


def row_places():
    tables = []
    for core in range(2):
        masks = [m[core] for m in FIRST]
        table = []
        for p in range(16):
            rel = 0
            for bit in range(4):
                rel ^= masks[bit] if p >> bit & 1 else 0
            table.append(rel)
        tables.append(table)
    core = lax.axis_index("row") % 2
    table = jnp.where(core == 0, jnp.array(tables[0], jnp.int32), jnp.array(tables[1], jnp.int32))
    return table ^ lax.axis_index("col").astype(jnp.int32)


def col_places():
    tables = []
    for core in range(2):
        table = []
        for k in range(4):
            for sibling in range(2):
                of = core ^ sibling
                z = (ZA[of] if k & 1 else 0) ^ (ZB[of] if k & 2 else 0)
                table.append(z * 2 + sibling)
        tables.append(table + [0])
    row = lax.axis_index("row").astype(jnp.int32)
    table = jnp.where(row % 2 == 0, jnp.array(tables[0], jnp.int32), jnp.array(tables[1], jnp.int32))
    return table ^ row


def second(p):
    return (p & 5) << 1 | (p & 10) >> 1


def vmem(count):
    return [pl.BlockSpec(memory_space=pltpu.VMEM)] * count


def smem(count):
    return [pl.BlockSpec(memory_space=pltpu.SMEM)] * count


def call(body, outs, places=0, arrays=0, scratch=(), flops=0, moved=0, limit=LIMIT, far=0, far_out=0):
    out_specs = jax.tree.map(lambda _: pl.BlockSpec(memory_space=pltpu.VMEM), outs)
    if far_out:
        out_specs = out_specs[:-far_out] + (pl.BlockSpec(memory_space=pltpu.HBM),) * far_out
    return pl.pallas_call(
        body,
        out_shape=outs,
        in_specs=smem(places) + [pl.BlockSpec(memory_space=pltpu.HBM)] * far + vmem(arrays),
        out_specs=out_specs,
        scratch_shapes=list(scratch),
        compiler_params=pltpu.CompilerParams(vmem_limit_bytes=limit * 2**20),
        cost_estimate=pl.CostEstimate(flops=flops, bytes_accessed=moved, transcendentals=0),
    )


def shape(dims, dtype=F32):
    return jax.ShapeDtypeStruct(dims, dtype)


def split(value):
    high = value.astype(BF)
    return high, (value - high.astype(F32)).astype(BF)


def diagonal():
    one = lax.broadcasted_iota(jnp.int32, (128, 128), 0)
    return one == lax.broadcasted_iota(jnp.int32, (128, 128), 1)


def compact(ref):
    eye = diagonal()
    return jnp.concatenate(
        [
            jnp.sum(jnp.where(eye, ref[128 * q : 128 * q + 128, :], 0.0), axis=0, keepdims=True)
            for q in range(4)
        ],
        axis=0,
    )


def spread(value, ref):
    eye = diagonal()
    for q in range(4):
        wide = jnp.broadcast_to(value[q : q + 1, :], (128, 128))
        column = jnp.sum(jnp.where(eye, wide, 0.0), axis=1, keepdims=True)
        ref[128 * q : 128 * q + 128, :] = jnp.broadcast_to(column, (128, 128))


def block(p):
    return pl.ds(32 * p, 32)


def place(places, p):
    return pl.ds(pl.multiple_of(places[p] * 32, 32), 32)


def dot_t(one, two):
    return lax.dot_general(one, two, (((1,), (1,)), ((), ())), preferred_element_type=F32)


def group(k, pieces, high, low, norm):
    for at, ref in ((0, pieces[2 * k]), (128, pieces[2 * k + 1])):
        for p in range(4):
            rows = slice(256 * k + at + 32 * p, 256 * k + at + 32 * p + 32)
            value = ref[32 * p : 32 * p + 32, :]
            high[rows, :], low[rows, :] = split(value)
            total = jnp.sum(value * value, axis=1, keepdims=True)
            norm[at + 32 * p : at + 32 * p + 32, :] = jnp.broadcast_to(total, (32, 128))


def score(k, scale, terms, nn, high, low, norm, out, lanes):
    eye = diagonal()
    norms = jnp.concatenate(
        [
            jnp.sum(jnp.where(eye, norm[128 * q : 128 * q + 128, :], 0.0), axis=0, keepdims=True)
            for q in range(2)
        ],
        axis=1,
    )
    cols = slice(256 * k, 256 * k + 256)
    both = dot_t(terms[...], high[cols, :])
    cross = both[:ROWS] + both[ROWS:] + dot_t(terms[:ROWS, :], low[cols, :])
    out[:, lanes] = (2.0 * cross - nn[:, :1] - norms) * scale


def data_body(*refs):
    pieces, norms, (dh, dl), (high, low, outs) = refs[:6], refs[6], refs[7:9], refs[9:]
    sent = []
    for k in range(3):
        group(k, pieces, high, low, norms.at[256 * k : 256 * k + 256, :])
        rows = slice(256 * k, 256 * k + 256)
        for i, (source, target) in enumerate(((high, dh), (low, dl))):
            sent.append(
                pltpu.make_async_copy(source.at[rows, :], target.at[rows, :], outs.at[2 * k + i])
            )
            sent[-1].start()
    for copy in sent:
        copy.wait()


def row_sums(value):
    peak = jnp.max(value, axis=1, keepdims=True)
    total = jnp.sum(jnp.exp(value - peak), axis=1, keepdims=True)
    return jnp.broadcast_to(peak, (32, 128)), jnp.broadcast_to(total, (32, 128))


def early_body(scale, *refs):
    data, norms, noise = refs[0:2], refs[2], refs[3:7]
    terms, nn, scores, peaks, totals = refs[7:12]
    high, low, sems = refs[12:]
    copies = []
    for k in range(3):
        rows = slice(256 * k, 256 * k + 256)
        for i, (source, target) in enumerate(zip(data, (high, low))):
            copies.append(
                pltpu.make_async_copy(source.at[rows, :], target.at[rows, :], sems.at[2 * k + i])
            )
            copies[-1].start()
    middle = noise[0].shape[1]
    for p in range(16):
        q = second(p)
        one = noise[p // 8][32 * (p % 8) : 32 * (p % 8) + 32, :]
        two = noise[2 + q // 8][32 * (q % 8) : 32 * (q % 8) + 32, :]
        top, under = slice(32 * p, 32 * p + 32), slice(ROWS + 32 * p, ROWS + 32 * p + 32)
        terms[top, :middle], terms[under, :middle] = split(one)
        terms[top, middle:], terms[under, middle:] = split(two)
        total = jnp.sum(one * one + two * two, axis=1, keepdims=True)
        nn[32 * p : 32 * p + 32, :] = jnp.broadcast_to(total, (32, 128))
    for copy in copies:
        copy.wait()
    for k in range(3):
        rows = slice(256 * k, 256 * k + 256)
        score(k, scale, terms, nn, high, low, norms.at[rows, :], scores, rows)
    for p in range(16):
        peaks[block(p), :], totals[block(p), :] = row_sums(scores[block(p), :])


def late_body(scale, places, own, sibling, terms, nn, peaks, totals, scores, out, dh, dl, *scratch):
    high, low, norm, ends, sums, sems = scratch
    group(0, (own, sibling), high, low, norm)
    sent = [
        pltpu.make_async_copy(source, target, sems.at[i])
        for i, (source, target) in enumerate(((high, dh), (low, dl)))
    ]
    for copy in sent:
        copy.start()
    score(0, scale, terms, nn, high, low, norm, scores, slice(0, 256))
    for p in range(16):
        peak, total = row_sums(scores[block(p), :])
        before = peaks[block(p), :]
        top = jnp.maximum(peak, before)
        ends[place(places, p), :] = top
        sums[place(places, p), :] = total * jnp.exp(peak - top) + totals[block(p), :] * jnp.exp(
            before - top
        )
    value = jnp.concatenate([compact(ends), compact(sums)], axis=0)
    for to in range(16):
        out[to] = value
    for copy in sent:
        copy.wait()


def col_first_body(rplaces, cplaces, got, early, late, plan, out, pots, ends):
    peak = got[0, 0:4, :]
    for one in range(1, 16):
        peak = jnp.maximum(peak, got[one, 0:4, :])
    total = got[0, 4:8, :] * jnp.exp(got[0, 0:4, :] - peak)
    for one in range(1, 16):
        total = total + got[one, 4:8, :] * jnp.exp(got[one, 0:4, :] - peak)
    spread(math.log(DATA) - (peak + jnp.log(total)), pots)
    for k in range(4):
        lanes = slice(256 * k, 256 * k + 256)
        high = None
        for p in range(16):
            value = late[block(p), :] if k == 3 else early[block(p), lanes]
            value = value + pots[place(rplaces, p), :][:, :1]
            plan[block(p), lanes] = value
            value = jnp.max(value.reshape(4, 8, 256), axis=0)
            high = value if high is None else jnp.maximum(high, value)
        high = jnp.max(high, axis=0, keepdims=True)
        sums = None
        for p in range(16):
            value = jnp.exp(plan[block(p), lanes] - high)
            plan[block(p), lanes] = value
            value = jnp.sum(value.reshape(4, 8, 256), axis=0)
            sums = value if sums is None else sums + value
        sums = jnp.sum(sums, axis=0, keepdims=True)
        for half in range(2):
            at = cplaces[2 * k + half]
            ends[pl.ds(at, 1), :] = high[:, 128 * half : 128 * half + 128]
            ends[pl.ds(8 + at, 1), :] = sums[:, 128 * half : 128 * half + 128]
    for to in range(8):
        out[to] = ends[...]


def to_lanes(cplaces, ref):
    return jnp.concatenate([ref[pl.ds(cplaces[b], 1), :] for b in range(8)], axis=1)


def row_second_body(rplaces, cplaces, got, plan, out, gains, totals):
    high = got[0, 0:8, :]
    for one in range(1, 8):
        high = jnp.maximum(high, got[one, 0:8, :])
    total = got[0, 8:16, :] * jnp.exp(got[0, 0:8, :] - high)
    for one in range(1, 8):
        total = total + got[one, 8:16, :] * jnp.exp(got[one, 0:8, :] - high)
    own = got[pl.ds(cplaces[8], 1)][0, 0:8, :]
    gains[...] = NOISE * jnp.exp(own - high) / total
    lanes = to_lanes(cplaces, gains)
    for p in range(16):
        value = jnp.sum(plan[block(p), :] * lanes, axis=1, keepdims=True)
        totals[place(rplaces, p), :] = jnp.broadcast_to(value, (32, 128))
    value = compact(totals)
    value = jnp.concatenate([value, value], axis=0)
    for to in range(16):
        out[to] = value


def col_second_body(rplaces, cplaces, got, gains, plan, out, scales, ends):
    total = got[0, 0:4, :]
    for one in range(1, 16):
        total = total + got[one, 0:4, :]
    spread(DATA / total, scales)
    sums = None
    for p in range(16):
        value = plan[block(p), :] * scales[place(rplaces, p), :][:, :1]
        value = jnp.sum(value.reshape(4, 8, COLS), axis=0)
        sums = value if sums is None else sums + value
    sums = jnp.sum(sums, axis=0, keepdims=True)
    for b in range(8):
        ends[pl.ds(cplaces[b], 1), :] = sums[:, 128 * b : 128 * b + 128]
    value = ends[...] * gains[...]
    for to in range(8):
        out[to] = value


def weight_body(cplaces, got, gains, plan, high, low, denom, ends, totals):
    total = got[0]
    for one in range(1, 8):
        total = total + got[one]
    ends[...] = gains[...] * (NOISE / total)
    lanes = to_lanes(cplaces, ends)
    for p in range(16):
        value = plan[block(p), :] * lanes
        high[block(p), :], low[block(p), :] = split(value)
        totals[block(p), :] = jnp.broadcast_to(jnp.sum(value, axis=1, keepdims=True), (32, 128))
    denom[...] = totals[...]


def dot(one, two):
    return jnp.dot(one, two, preferred_element_type=F32)


def product_body(blocks, chunks, wh, wl, denom, h0, l0, h1, l1, *outs):
    terms = [
        jnp.concatenate([ref[block(p), at] for ref in (wh, wl) for p in blocks], axis=0)
        for at in (slice(0, 768), slice(768, 1024))
    ]
    for chunk, out in zip(chunks, outs):
        for n in range(2):
            at = slice(512 * chunk + 256 * n, 512 * chunk + 256 * n + 256)
            both = dot(terms[0], h0[:, at]) + dot(terms[1], h1[:, at])
            more = dot(terms[0][:256], l0[:, at]) + dot(terms[1][:256], l1[:, at])
            total = both[:256] + both[256:] + more
            for i in range(8):
                for t in range(2):
                    tile = total[32 * i : 32 * i + 32, 128 * t : 128 * t + 128]
                    out[i, 32 * (2 * n + t) : 32 * (2 * n + t) + 32, :] = tile
        if chunk == 0:
            eye = diagonal()[:32, :]
            for i, p in enumerate(blocks):
                row = jnp.sum(jnp.where(eye, denom[block(p), :], 0.0), axis=0, keepdims=True)
                out[i, 128:136, :] = jnp.broadcast_to(row, (8, 128))


def end_body(left, right, noise, times, path, velocity):
    eye = diagonal()[:32, :]
    wide = jnp.broadcast_to(left[0, 128:129, :], (32, 128))
    inverse = 1.0 / jnp.sum(jnp.where(eye, wide, 0.0), axis=1, keepdims=True)
    for side, (ref, starts) in enumerate(((left, (0, 136)), (right, (0, 128)))):
        for t in range(8):
            lanes = slice(1024 * side + 128 * t, 1024 * side + 128 * t + 128)
            first = starts[t // 4] + 32 * (t % 4)
            target = ref[0, first : first + 32, :] * inverse
            own = noise[:, lanes]
            at = times[:, :1]
            path[:, lanes] = (1.0 - at) * own + at * target
            velocity[:, lanes] = target - own


def after(*values):
    return lax.optimization_barrier(values)


def product(blocks, chunks, *arrays):
    return call(
        lambda *refs: product_body(blocks, chunks, *refs),
        tuple(shape((8, 136 if chunk == 0 else 128, 128)) for chunk in chunks),
        0,
        7,
    )(*arrays)


ORDER_1 = list(range(16))
ORDER_2 = [second(p) for p in ORDER_1]


def per_device(noise, data, times):
    features = noise.shape[1]
    middle = features // 2
    scale = 1.0 / (features * EPS)
    rplaces, cplaces = row_places(), col_places()

    near, far = swap_z(data, ZA), swap_z(data, ZB)
    parts = [noise[:, :middle], noise[:, middle:]]
    orders = (FIRST, SECOND)
    stages = []
    for step in range(3):
        parts = [
            jnp.concatenate([part, swap_col(part, order[step])], axis=0)
            for part, order in zip(parts, orders)
        ]
        stages.append(parts)
    last = [swap_col(part, order[3]) for part, order in zip(parts, orders)]
    first = data
    near = after(near, *stages[1])[0]
    own = [data, near, far, swap_z(near, ZB)]
    cross = [swap_core(first), swap_core(near), swap_core(far), swap_core(own[3])]
    pieces = [[part, one] for part, one in zip(parts, last)]

    wide = pltpu.VMEM((ROWS, 128), F32)
    norms, h0, l0 = call(
        data_body,
        (shape((768, 128)),) + (shape((768, features), BF),) * 2,
        arrays=6,
        scratch=(
            pltpu.VMEM((768, features), BF),
            pltpu.VMEM((768, features), BF),
            pltpu.SemaphoreType.DMA((6,)),
        ),
        moved=12 * 2**20,
        far_out=2,
    )(own[0], cross[0], own[1], cross[1], own[2], cross[2])
    rows, row_norms, early, peaks, totals = call(
        lambda *refs: early_body(scale, *refs),
        (shape((2 * ROWS, features), BF), shape((ROWS, 128)), shape((ROWS, 768)))
        + (shape((ROWS, 128)),) * 2,
        arrays=5,
        scratch=(
            pltpu.VMEM((768, features), BF),
            pltpu.VMEM((768, features), BF),
            pltpu.SemaphoreType.DMA((6,)),
        ),
        flops=3 * 2 * ROWS * 768 * features,
        moved=16 * 2**20,
        limit=20,
        far=2,
    )(h0, l0, norms, *pieces[0], *pieces[1])
    late, send, h1, l1 = call(
        lambda *refs: late_body(scale, *refs),
        (shape((ROWS, 256)), shape((16, 8, 128))) + (shape((256, features), BF),) * 2,
        1,
        6,
        scratch=(
            pltpu.VMEM((256, features), BF),
            pltpu.VMEM((256, features), BF),
            pltpu.VMEM((256, 128), F32),
            wide,
            wide,
            pltpu.SemaphoreType.DMA((2,)),
        ),
        flops=3 * 2 * ROWS * 256 * features,
        moved=8 * 2**20,
        far_out=2,
    )(rplaces, own[3], cross[3], rows, row_norms, peaks, totals)
    send, rplaces, cplaces = after(send, rplaces, cplaces)
    got = lax.all_to_all(send, "col", 0, 0)
    plan, send = call(
        col_first_body,
        (shape((ROWS, COLS)), shape((8, 16, 128))),
        2,
        3,
        (wide, pltpu.VMEM((16, 128), F32)),
    )(rplaces, cplaces, got, early, late)
    got = lax.all_to_all(send, "row", 0, 0)
    send, gains = call(
        row_second_body,
        (shape((16, 8, 128)), shape((8, 128))),
        2,
        2,
        (wide,),
    )(rplaces, cplaces, got, plan)
    got = lax.all_to_all(send, "col", 0, 0)
    send = call(
        col_second_body,
        shape((8, 8, 128)),
        2,
        3,
        (wide, pltpu.VMEM((8, 128), F32)),
    )(rplaces, cplaces, got, gains, plan)
    got = lax.all_to_all(send, "row", 0, 0)
    wh, wl, denom = call(
        weight_body,
        (shape((ROWS, COLS), BF), shape((ROWS, COLS), BF), shape((ROWS, 128))),
        1,
        3,
        (pltpu.VMEM((8, 128), F32), wide),
    )(cplaces, got, gains, plan)

    rest = (wh, wl, denom, h0, l0, h1, l1)
    halves = ((ORDER_1, (0, 1), FIRST[::-1]), (ORDER_2, (2, 3), SECOND[::-1]))
    leaving = {}
    for i in range(2):
        for blocks, chunks, steps in halves:
            (out,) = product(blocks[8:], (chunks[i],), *rest)
            out, *rest = after(out, *rest)
            leaving[chunks[i]] = swap_col(out, steps[0])
    sums = {}
    for blocks, chunks, steps in halves:
        out = product(blocks[:8], chunks, *rest)
        *out, denom = after(*out, rest[2])
        rest = (rest[0], rest[1], denom) + tuple(rest[3:])
        sums.update(zip(chunks, out))
    order = [(chunks[i], steps) for i in range(2) for _, chunks, steps in halves]
    last = rest[2]
    for chunk, steps in order:
        sums[chunk] = last = sums[chunk] + after(leaving[chunk], last)[0]
        leaving[chunk] = swap_col(last[4:], steps[1])
    for chunk, steps in order:
        sums[chunk] = last = sums[chunk][:4] + after(leaving[chunk], last)[0]
    ends = [
        jnp.concatenate([sums[chunk] for chunk in chunks], axis=1) for _, chunks, _ in halves
    ]
    for step, rows in ((2, 2), (3, 1)):
        coming = [swap_col(end[rows:], half[2][step]) for end, half in zip(ends, halves)]
        for i in range(2):
            ends[i] = last = ends[i][:rows] + after(coming[i], last)[0]
    left, right = ends
    wide_times = jnp.broadcast_to(times[:, None], (times.shape[0], 128))
    outs = (shape(noise.shape), shape(noise.shape))
    return call(end_body, outs, 0, 4)(left, right, noise, wide_times)


def solution(mesh):
    in_specs = (P(("row", "col"), None), P(("col", "row"), None), P(("row", "col")))
    out_specs = (P(("row", "col"), None), P(("row", "col"), None))
    return jax.shard_map(
        per_device, mesh=mesh, in_specs=in_specs, out_specs=out_specs, check_vma=False
    )
```

```python
import math

import jax
import jax.numpy as jnp
from jax import lax
from jax.experimental import pallas as pl
from jax.experimental.pallas import tpu as pltpu
from jax.sharding import PartitionSpec as P

EPS = 0.05
LIMIT = 14
BOTH = ("row", "col")
NOISE, DATA = 4096, 16384
ROWS, COLS = 512, 1024
BF, F32 = jnp.bfloat16, jnp.float32

UA, UB, VA, VB, VC = (1, 4), (3, 12), (4, 1), (12, 3), (8, 2)
FIRST, SECOND = (VA, VB, UA, UB), (VB, VA, UB, UA)
ZA, ZB = (1, 3), (3, 1)


def swap_col(value, masks):
    pairs = [
        (row * 16 + col, row * 16 + (col ^ masks[row % 2])) for row in range(8) for col in range(16)
    ]
    return lax.ppermute(value, BOTH, pairs)


def swap_z(value, masks):
    pairs = [
        (row * 16 + col, (row ^ (2 * masks[row % 2])) * 16 + col)
        for row in range(8)
        for col in range(16)
    ]
    return lax.ppermute(value, BOTH, pairs)


def swap_core(value):
    return lax.ppermute(value, "row", [(row, row ^ 1) for row in range(8)])


def row_places():
    tables = []
    for core in range(2):
        masks = [m[core] for m in FIRST]
        table = []
        for p in range(16):
            rel = 0
            for bit in range(4):
                rel ^= masks[bit] if p >> bit & 1 else 0
            table.append(rel)
        tables.append(table)
    core = lax.axis_index("row") % 2
    table = jnp.where(core == 0, jnp.array(tables[0], jnp.int32), jnp.array(tables[1], jnp.int32))
    return table ^ lax.axis_index("col").astype(jnp.int32)


def col_places():
    tables = []
    for core in range(2):
        table = []
        for k in range(4):
            for sibling in range(2):
                of = core ^ sibling
                z = (ZA[of] if k & 1 else 0) ^ (ZB[of] if k & 2 else 0)
                table.append(z * 2 + sibling)
        tables.append(table + [0])
    row = lax.axis_index("row").astype(jnp.int32)
    table = jnp.where(row % 2 == 0, jnp.array(tables[0], jnp.int32), jnp.array(tables[1], jnp.int32))
    return table ^ row


def second(p):
    return (p & 5) << 1 | (p & 10) >> 1


def vmem(count):
    return [pl.BlockSpec(memory_space=pltpu.VMEM)] * count


def smem(count):
    return [pl.BlockSpec(memory_space=pltpu.SMEM)] * count


def call(body, outs, places=0, arrays=0, scratch=(), flops=0, moved=0, limit=LIMIT, far=0, far_out=0):
    out_specs = jax.tree.map(lambda _: pl.BlockSpec(memory_space=pltpu.VMEM), outs)
    if far_out:
        out_specs = out_specs[:-far_out] + (pl.BlockSpec(memory_space=pltpu.HBM),) * far_out
    return pl.pallas_call(
        body,
        out_shape=outs,
        in_specs=smem(places) + [pl.BlockSpec(memory_space=pltpu.HBM)] * far + vmem(arrays),
        out_specs=out_specs,
        scratch_shapes=list(scratch),
        compiler_params=pltpu.CompilerParams(vmem_limit_bytes=limit * 2**20),
        cost_estimate=pl.CostEstimate(flops=flops, bytes_accessed=moved, transcendentals=0),
    )


def shape(dims, dtype=F32):
    return jax.ShapeDtypeStruct(dims, dtype)


def split(value):
    high = value.astype(BF)
    return high, (value - high.astype(F32)).astype(BF)


def diagonal():
    one = lax.broadcasted_iota(jnp.int32, (128, 128), 0)
    return one == lax.broadcasted_iota(jnp.int32, (128, 128), 1)


def compact(ref):
    eye = diagonal()
    return jnp.concatenate(
        [
            jnp.sum(jnp.where(eye, ref[128 * q : 128 * q + 128, :], 0.0), axis=0, keepdims=True)
            for q in range(4)
        ],
        axis=0,
    )


def spread(value, ref):
    eye = diagonal()
    for q in range(4):
        wide = jnp.broadcast_to(value[q : q + 1, :], (128, 128))
        column = jnp.sum(jnp.where(eye, wide, 0.0), axis=1, keepdims=True)
        ref[128 * q : 128 * q + 128, :] = jnp.broadcast_to(column, (128, 128))


def block(p):
    return pl.ds(32 * p, 32)


def place(places, p):
    return pl.ds(pl.multiple_of(places[p] * 32, 32), 32)


def dot_t(one, two):
    return lax.dot_general(one, two, (((1,), (1,)), ((), ())), preferred_element_type=F32)


def group(k, pair, high, low, norm):
    for at, ref in ((0, pair[0]), (128, pair[1])):
        for p in range(4):
            rows = slice(256 * k + at + 32 * p, 256 * k + at + 32 * p + 32)
            value = ref[32 * p : 32 * p + 32, :]
            high[rows, :], low[rows, :] = split(value)
            total = jnp.sum(value * value, axis=1, keepdims=True)
            norm[at + 32 * p : at + 32 * p + 32, :] = jnp.broadcast_to(total, (32, 128))


def score(k, scale, terms, nn, high, low, norm, out, lanes):
    eye = diagonal()
    norms = jnp.concatenate(
        [
            jnp.sum(jnp.where(eye, norm[128 * q : 128 * q + 128, :], 0.0), axis=0, keepdims=True)
            for q in range(2)
        ],
        axis=1,
    )
    cols = slice(256 * k, 256 * k + 256)
    both = dot_t(terms[...], high[cols, :])
    cross = both[:ROWS] + both[ROWS:] + dot_t(terms[:ROWS, :], low[cols, :])
    out[:, lanes] = (2.0 * cross - nn[:, :1] - norms) * scale


def data_body(*refs):
    data, norms, (dh, dl), (pieces, high, low, sems, outs) = refs[:6], refs[6], refs[7:9], refs[9:]
    copies = [pltpu.make_async_copy(ref, pieces.at[i], sems.at[i]) for i, ref in enumerate(data)]
    for copy in copies:
        copy.start()
    sent = []
    for k in range(3):
        copies[2 * k].wait()
        copies[2 * k + 1].wait()
        both = [pieces.at[2 * k + i] for i in range(2)]
        group(k, both, high, low, norms.at[256 * k : 256 * k + 256, :])
        rows = slice(256 * k, 256 * k + 256)
        for i, (source, target) in enumerate(((high, dh), (low, dl))):
            sent.append(
                pltpu.make_async_copy(source.at[rows, :], target.at[rows, :], outs.at[2 * k + i])
            )
            sent[-1].start()
    for copy in sent:
        copy.wait()


def row_sums(value):
    peak = jnp.max(value, axis=1, keepdims=True)
    total = jnp.sum(jnp.exp(value - peak), axis=1, keepdims=True)
    return jnp.broadcast_to(peak, (32, 128)), jnp.broadcast_to(total, (32, 128))


def early_body(scale, *refs):
    data, norms, noise = refs[0:2], refs[2], refs[3:7]
    terms, nn, scores, peaks, totals = refs[7:12]
    high, low, sems = refs[12:]
    copies = []
    for k in range(3):
        rows = slice(256 * k, 256 * k + 256)
        for i, (source, target) in enumerate(zip(data, (high, low))):
            copies.append(
                pltpu.make_async_copy(source.at[rows, :], target.at[rows, :], sems.at[2 * k + i])
            )
            copies[-1].start()
    middle = noise[0].shape[1]
    for p in range(16):
        q = second(p)
        one = noise[p // 8][32 * (p % 8) : 32 * (p % 8) + 32, :]
        two = noise[2 + q // 8][32 * (q % 8) : 32 * (q % 8) + 32, :]
        top, under = slice(32 * p, 32 * p + 32), slice(ROWS + 32 * p, ROWS + 32 * p + 32)
        terms[top, :middle], terms[under, :middle] = split(one)
        terms[top, middle:], terms[under, middle:] = split(two)
        total = jnp.sum(one * one + two * two, axis=1, keepdims=True)
        nn[32 * p : 32 * p + 32, :] = jnp.broadcast_to(total, (32, 128))
    for copy in copies:
        copy.wait()
    for k in range(3):
        rows = slice(256 * k, 256 * k + 256)
        score(k, scale, terms, nn, high, low, norms.at[rows, :], scores, rows)
    for p in range(16):
        peaks[block(p), :], totals[block(p), :] = row_sums(scores[block(p), :])


def late_body(scale, places, own, sibling, terms, nn, peaks, totals, scores, out, dh, dl, *scratch):
    high, low, norm, ends, sums, sems = scratch
    group(0, (own, sibling), high, low, norm)
    sent = [
        pltpu.make_async_copy(source, target, sems.at[i])
        for i, (source, target) in enumerate(((high, dh), (low, dl)))
    ]
    for copy in sent:
        copy.start()
    score(0, scale, terms, nn, high, low, norm, scores, slice(0, 256))
    for p in range(16):
        peak, total = row_sums(scores[block(p), :])
        before = peaks[block(p), :]
        top = jnp.maximum(peak, before)
        ends[place(places, p), :] = top
        sums[place(places, p), :] = total * jnp.exp(peak - top) + totals[block(p), :] * jnp.exp(
            before - top
        )
    value = jnp.concatenate([compact(ends), compact(sums)], axis=0)
    for to in range(16):
        out[to] = value
    for copy in sent:
        copy.wait()


def col_first_body(rplaces, cplaces, got, early, late, plan, out, pots, ends):
    peak = got[0, 0:4, :]
    for one in range(1, 16):
        peak = jnp.maximum(peak, got[one, 0:4, :])
    total = got[0, 4:8, :] * jnp.exp(got[0, 0:4, :] - peak)
    for one in range(1, 16):
        total = total + got[one, 4:8, :] * jnp.exp(got[one, 0:4, :] - peak)
    spread(math.log(DATA) - (peak + jnp.log(total)), pots)
    for k in range(4):
        lanes = slice(256 * k, 256 * k + 256)
        high = None
        for p in range(16):
            value = late[block(p), :] if k == 3 else early[block(p), lanes]
            value = value + pots[place(rplaces, p), :][:, :1]
            plan[block(p), lanes] = value
            value = jnp.max(value.reshape(4, 8, 256), axis=0)
            high = value if high is None else jnp.maximum(high, value)
        high = jnp.max(high, axis=0, keepdims=True)
        sums = None
        for p in range(16):
            value = jnp.exp(plan[block(p), lanes] - high)
            plan[block(p), lanes] = value
            value = jnp.sum(value.reshape(4, 8, 256), axis=0)
            sums = value if sums is None else sums + value
        sums = jnp.sum(sums, axis=0, keepdims=True)
        for half in range(2):
            at = cplaces[2 * k + half]
            ends[pl.ds(at, 1), :] = high[:, 128 * half : 128 * half + 128]
            ends[pl.ds(8 + at, 1), :] = sums[:, 128 * half : 128 * half + 128]
    for to in range(8):
        out[to] = ends[...]


def to_lanes(cplaces, ref):
    return jnp.concatenate([ref[pl.ds(cplaces[b], 1), :] for b in range(8)], axis=1)


def row_second_body(rplaces, cplaces, got, plan, out, gains, totals):
    high = got[0, 0:8, :]
    for one in range(1, 8):
        high = jnp.maximum(high, got[one, 0:8, :])
    total = got[0, 8:16, :] * jnp.exp(got[0, 0:8, :] - high)
    for one in range(1, 8):
        total = total + got[one, 8:16, :] * jnp.exp(got[one, 0:8, :] - high)
    own = got[pl.ds(cplaces[8], 1)][0, 0:8, :]
    gains[...] = NOISE * jnp.exp(own - high) / total
    lanes = to_lanes(cplaces, gains)
    for p in range(16):
        value = jnp.sum(plan[block(p), :] * lanes, axis=1, keepdims=True)
        totals[place(rplaces, p), :] = jnp.broadcast_to(value, (32, 128))
    value = compact(totals)
    value = jnp.concatenate([value, value], axis=0)
    for to in range(16):
        out[to] = value


def col_second_body(rplaces, cplaces, got, gains, plan, out, scales, ends):
    total = got[0, 0:4, :]
    for one in range(1, 16):
        total = total + got[one, 0:4, :]
    spread(DATA / total, scales)
    sums = None
    for p in range(16):
        value = plan[block(p), :] * scales[place(rplaces, p), :][:, :1]
        value = jnp.sum(value.reshape(4, 8, COLS), axis=0)
        sums = value if sums is None else sums + value
    sums = jnp.sum(sums, axis=0, keepdims=True)
    for b in range(8):
        ends[pl.ds(cplaces[b], 1), :] = sums[:, 128 * b : 128 * b + 128]
    value = ends[...] * gains[...]
    for to in range(8):
        out[to] = value


def weight_body(cplaces, got, gains, plan, high, low, denom, ends, totals):
    total = got[0]
    for one in range(1, 8):
        total = total + got[one]
    ends[...] = gains[...] * (NOISE / total)
    lanes = to_lanes(cplaces, ends)
    for p in range(16):
        value = plan[block(p), :] * lanes
        high[block(p), :], low[block(p), :] = split(value)
        totals[block(p), :] = jnp.broadcast_to(jnp.sum(value, axis=1, keepdims=True), (32, 128))
    denom[...] = totals[...]


def dot(one, two):
    return jnp.dot(one, two, preferred_element_type=F32)


def product_body(blocks, chunks, wh, wl, denom, h0, l0, h1, l1, *outs):
    terms = [
        jnp.concatenate([ref[block(p), at] for ref in (wh, wl) for p in blocks], axis=0)
        for at in (slice(0, 768), slice(768, 1024))
    ]
    for chunk, out in zip(chunks, outs):
        for n in range(2):
            at = slice(512 * chunk + 256 * n, 512 * chunk + 256 * n + 256)
            both = dot(terms[0], h0[:, at]) + dot(terms[1], h1[:, at])
            more = dot(terms[0][:256], l0[:, at]) + dot(terms[1][:256], l1[:, at])
            total = both[:256] + both[256:] + more
            for i in range(8):
                for t in range(2):
                    tile = total[32 * i : 32 * i + 32, 128 * t : 128 * t + 128]
                    out[i, 32 * (2 * n + t) : 32 * (2 * n + t) + 32, :] = tile
        if chunk == 0:
            eye = diagonal()[:32, :]
            for i, p in enumerate(blocks):
                row = jnp.sum(jnp.where(eye, denom[block(p), :], 0.0), axis=0, keepdims=True)
                out[i, 128:136, :] = jnp.broadcast_to(row, (8, 128))


def end_body(one, two, three, four, noise, times, path, velocity):
    eye = diagonal()[:32, :]

    def total(rows):
        return (one[rows, :] + two[rows, :]) + (three[rows, :] + four[rows, :])

    wide = jnp.broadcast_to(total(slice(128, 136))[:1, :], (32, 128))
    inverse = 1.0 / jnp.sum(jnp.where(eye, wide, 0.0), axis=1, keepdims=True)
    for t in range(16):
        lanes = slice(128 * t, 128 * t + 128)
        first = 32 * t + (0 if t < 4 else 8)
        target = total(slice(first, first + 32)) * inverse
        own = noise[:, lanes]
        at = times[:, :1]
        path[:, lanes] = (1.0 - at) * own + at * target
        velocity[:, lanes] = target - own


def after(*values):
    return lax.optimization_barrier(values)


def product(blocks, chunks, *arrays):
    return call(
        lambda *refs: product_body(blocks, chunks, *refs),
        tuple(shape((8, 136 if chunk == 0 else 128, 128)) for chunk in chunks),
        0,
        7,
    )(*arrays)


ORDER_1 = list(range(16))
ORDER_2 = [second(p) for p in ORDER_1]


def per_device(noise, data, times):
    features = noise.shape[1]
    middle = features // 2
    scale = 1.0 / (features * EPS)
    rplaces, cplaces = row_places(), col_places()

    near, far = swap_z(data, ZA), swap_z(data, ZB)
    parts = [noise[:, :middle], noise[:, middle:]]
    orders = (FIRST, SECOND)
    stages = []
    for step in range(3):
        parts = [
            jnp.concatenate([part, swap_col(part, order[step])], axis=0)
            for part, order in zip(parts, orders)
        ]
        stages.append(parts)
    last = [swap_col(part, order[3]) for part, order in zip(parts, orders)]
    first = data
    near = after(near, *stages[1])[0]
    own = [data, near, far, swap_z(near, ZB)]
    cross = [swap_core(first), swap_core(near), swap_core(far), swap_core(own[3])]
    pieces = [[part, one] for part, one in zip(parts, last)]

    wide = pltpu.VMEM((ROWS, 128), F32)
    norms, h0, l0 = call(
        data_body,
        (shape((768, 128)),) + (shape((768, features), BF),) * 2,
        scratch=(
            pltpu.VMEM((6, 128, features), F32),
            pltpu.VMEM((768, features), BF),
            pltpu.VMEM((768, features), BF),
            pltpu.SemaphoreType.DMA((6,)),
            pltpu.SemaphoreType.DMA((6,)),
        ),
        moved=12 * 2**20,
        far=6,
        far_out=2,
    )(own[0], cross[0], own[1], cross[1], own[2], cross[2])
    rows, row_norms, early, peaks, totals = call(
        lambda *refs: early_body(scale, *refs),
        (shape((2 * ROWS, features), BF), shape((ROWS, 128)), shape((ROWS, 768)))
        + (shape((ROWS, 128)),) * 2,
        arrays=5,
        scratch=(
            pltpu.VMEM((768, features), BF),
            pltpu.VMEM((768, features), BF),
            pltpu.SemaphoreType.DMA((6,)),
        ),
        flops=3 * 2 * ROWS * 768 * features,
        moved=16 * 2**20,
        limit=20,
        far=2,
    )(h0, l0, norms, *pieces[0], *pieces[1])
    late, send, h1, l1 = call(
        lambda *refs: late_body(scale, *refs),
        (shape((ROWS, 256)), shape((16, 8, 128))) + (shape((256, features), BF),) * 2,
        1,
        6,
        scratch=(
            pltpu.VMEM((256, features), BF),
            pltpu.VMEM((256, features), BF),
            pltpu.VMEM((256, 128), F32),
            wide,
            wide,
            pltpu.SemaphoreType.DMA((2,)),
        ),
        flops=3 * 2 * ROWS * 256 * features,
        moved=8 * 2**20,
        far_out=2,
    )(rplaces, own[3], cross[3], rows, row_norms, peaks, totals)
    send, rplaces, cplaces = after(send, rplaces, cplaces)
    got = lax.all_to_all(send, "col", 0, 0)
    plan, send = call(
        col_first_body,
        (shape((ROWS, COLS)), shape((8, 16, 128))),
        2,
        3,
        (wide, pltpu.VMEM((16, 128), F32)),
    )(rplaces, cplaces, got, early, late)
    got = lax.all_to_all(send, "row", 0, 0)
    send, gains = call(
        row_second_body,
        (shape((16, 8, 128)), shape((8, 128))),
        2,
        2,
        (wide,),
    )(rplaces, cplaces, got, plan)
    got = lax.all_to_all(send, "col", 0, 0)
    send = call(
        col_second_body,
        shape((8, 8, 128)),
        2,
        3,
        (wide, pltpu.VMEM((8, 128), F32)),
    )(rplaces, cplaces, got, gains, plan)
    got = lax.all_to_all(send, "row", 0, 0)
    wh, wl, denom = call(
        weight_body,
        (shape((ROWS, COLS), BF), shape((ROWS, COLS), BF), shape((ROWS, 128))),
        1,
        3,
        (pltpu.VMEM((8, 128), F32), wide),
    )(cplaces, got, gains, plan)

    rest = (wh, wl, denom, h0, l0, h1, l1)
    halves = ((ORDER_1, (0, 1), FIRST[::-1]), (ORDER_2, (2, 3), SECOND[::-1]))
    leaving = {}
    for i in range(2):
        for blocks, chunks, steps in halves:
            (out,) = product(blocks[8:], (chunks[i],), *rest)
            out, *rest = after(out, *rest)
            leaving[chunks[i]] = swap_col(out, steps[0])
    sums = {}
    for blocks, chunks, steps in halves:
        out = product(blocks[:8], chunks, *rest)
        *out, denom = after(*out, rest[2])
        rest = (rest[0], rest[1], denom) + tuple(rest[3:])
        sums.update(zip(chunks, out))
    order = [(chunks[i], steps) for i in range(2) for _, chunks, steps in halves]
    last = rest[2]
    for chunk, steps in order:
        sums[chunk] = last = sums[chunk] + after(leaving[chunk], last)[0]
        leaving[chunk] = swap_col(last[4:], steps[1])
    for chunk, steps in order:
        sums[chunk] = last = sums[chunk][:4] + after(leaving[chunk], last)[0]
    places = {(0, 0): (0, 0), VA: (1, 2), VB: (2, 1), VC: (3, 3)}

    def piece(masks):
        at = places[masks]
        return jnp.concatenate([sums[chunk][at[chunk // 2]] for chunk in range(4)], axis=0)

    parts = [piece((0, 0))] + [swap_col(piece(masks), masks) for masks in (VC, VA, VB)]
    wide_times = jnp.broadcast_to(times[:, None], (times.shape[0], 128))
    outs = (shape(noise.shape), shape(noise.shape))
    return call(end_body, outs, 0, 6)(*parts, noise, wide_times)


def solution(mesh):
    in_specs = (P(("row", "col"), None), P(("col", "row"), None), P(("row", "col")))
    out_specs = (P(("row", "col"), None), P(("row", "col"), None))
    return jax.shard_map(
        per_device, mesh=mesh, in_specs=in_specs, out_specs=out_specs, check_vma=False
    )
```

```python
import math

import jax
import jax.numpy as jnp
from jax import lax
from jax.experimental import pallas as pl
from jax.experimental.pallas import tpu as pltpu
from jax.sharding import PartitionSpec as P

EPS = 0.05
LIMIT = 14
BOTH = ("row", "col")
NOISE, DATA = 4096, 16384
ROWS, COLS = 512, 1024
BF, F32 = jnp.bfloat16, jnp.float32

UA, UB, VA, VB, VC = (1, 4), (3, 12), (4, 1), (12, 3), (8, 2)
FIRST, SECOND = (VA, VB, UA, UB), (VB, VA, UB, UA)
ZA, ZB = (1, 3), (3, 1)


def swap_col(value, masks):
    pairs = [
        (row * 16 + col, row * 16 + (col ^ masks[row % 2])) for row in range(8) for col in range(16)
    ]
    return lax.ppermute(value, BOTH, pairs)


def swap_z(value, masks):
    pairs = [
        (row * 16 + col, (row ^ (2 * masks[row % 2])) * 16 + col)
        for row in range(8)
        for col in range(16)
    ]
    return lax.ppermute(value, BOTH, pairs)


def swap_core(value):
    return lax.ppermute(value, "row", [(row, row ^ 1) for row in range(8)])


def row_places():
    tables = []
    for core in range(2):
        masks = [m[core] for m in FIRST]
        table = []
        for p in range(16):
            rel = 0
            for bit in range(4):
                rel ^= masks[bit] if p >> bit & 1 else 0
            table.append(rel)
        tables.append(table)
    core = lax.axis_index("row") % 2
    table = jnp.where(core == 0, jnp.array(tables[0], jnp.int32), jnp.array(tables[1], jnp.int32))
    return table ^ lax.axis_index("col").astype(jnp.int32)


def col_places():
    tables = []
    for core in range(2):
        table = []
        for k in range(4):
            for sibling in range(2):
                of = core ^ sibling
                z = (ZA[of] if k & 1 else 0) ^ (ZB[of] if k & 2 else 0)
                table.append(z * 2 + sibling)
        tables.append(table + [0])
    row = lax.axis_index("row").astype(jnp.int32)
    table = jnp.where(row % 2 == 0, jnp.array(tables[0], jnp.int32), jnp.array(tables[1], jnp.int32))
    return table ^ row


def second(p):
    return (p & 5) << 1 | (p & 10) >> 1


def vmem(count):
    return [pl.BlockSpec(memory_space=pltpu.VMEM)] * count


def smem(count):
    return [pl.BlockSpec(memory_space=pltpu.SMEM)] * count


def call(body, outs, places=0, arrays=0, scratch=(), flops=0, moved=0, limit=LIMIT, far=0, far_out=0):
    out_specs = jax.tree.map(lambda _: pl.BlockSpec(memory_space=pltpu.VMEM), outs)
    if far_out:
        out_specs = out_specs[:-far_out] + (pl.BlockSpec(memory_space=pltpu.HBM),) * far_out
    return pl.pallas_call(
        body,
        out_shape=outs,
        in_specs=smem(places) + [pl.BlockSpec(memory_space=pltpu.HBM)] * far + vmem(arrays),
        out_specs=out_specs,
        scratch_shapes=list(scratch),
        compiler_params=pltpu.CompilerParams(vmem_limit_bytes=limit * 2**20),
        cost_estimate=pl.CostEstimate(flops=flops, bytes_accessed=moved, transcendentals=0),
    )


def shape(dims, dtype=F32):
    return jax.ShapeDtypeStruct(dims, dtype)


def split(value):
    high = value.astype(BF)
    return high, (value - high.astype(F32)).astype(BF)


def diagonal():
    one = lax.broadcasted_iota(jnp.int32, (128, 128), 0)
    return one == lax.broadcasted_iota(jnp.int32, (128, 128), 1)


def compact(ref):
    eye = diagonal()
    return jnp.concatenate(
        [
            jnp.sum(jnp.where(eye, ref[128 * q : 128 * q + 128, :], 0.0), axis=0, keepdims=True)
            for q in range(4)
        ],
        axis=0,
    )


def spread(value, ref):
    eye = diagonal()
    for q in range(4):
        wide = jnp.broadcast_to(value[q : q + 1, :], (128, 128))
        column = jnp.sum(jnp.where(eye, wide, 0.0), axis=1, keepdims=True)
        ref[128 * q : 128 * q + 128, :] = jnp.broadcast_to(column, (128, 128))


def block(p):
    return pl.ds(32 * p, 32)


def place(places, p):
    return pl.ds(pl.multiple_of(places[p] * 32, 32), 32)


def dot_t(one, two):
    return lax.dot_general(one, two, (((1,), (1,)), ((), ())), preferred_element_type=F32)


def group(k, pair, high, low, norm):
    for at, ref in ((0, pair[0]), (128, pair[1])):
        for p in range(4):
            rows = slice(256 * k + at + 32 * p, 256 * k + at + 32 * p + 32)
            value = ref[32 * p : 32 * p + 32, :]
            high[rows, :], low[rows, :] = split(value)
            total = jnp.sum(value * value, axis=1, keepdims=True)
            norm[at + 32 * p : at + 32 * p + 32, :] = jnp.broadcast_to(total, (32, 128))


def score(k, scale, terms, nn, high, low, norm, out, lanes, half):
    eye = diagonal()
    norms = jnp.concatenate(
        [
            jnp.sum(jnp.where(eye, norm[128 * q : 128 * q + 128, :], 0.0), axis=0, keepdims=True)
            for q in range(2)
        ],
        axis=1,
    )
    cols = slice(256 * k, 256 * k + 256)
    rows = slice(256 * half, 256 * half + 256)
    top, under = terms[rows, :], terms[ROWS + 256 * half : ROWS + 256 * half + 256, :]
    cross = dot_t(top, high[cols, :]) + dot_t(under, high[cols, :]) + dot_t(top, low[cols, :])
    out[rows, lanes] = (2.0 * cross - nn[rows, :1] - norms) * scale


def data_body(*refs):
    data, norms, (dh, dl), (pieces, high, low, sems, outs) = refs[:6], refs[6], refs[7:9], refs[9:]
    copies = [pltpu.make_async_copy(ref, pieces.at[i], sems.at[i]) for i, ref in enumerate(data)]
    for copy in copies:
        copy.start()
    sent = []
    for k in range(3):
        copies[2 * k].wait()
        copies[2 * k + 1].wait()
        both = [pieces.at[2 * k + i] for i in range(2)]
        group(k, both, high, low, norms.at[256 * k : 256 * k + 256, :])
        rows = slice(256 * k, 256 * k + 256)
        for i, (source, target) in enumerate(((high, dh), (low, dl))):
            sent.append(
                pltpu.make_async_copy(source.at[rows, :], target.at[rows, :], outs.at[2 * k + i])
            )
            sent[-1].start()
    for copy in sent:
        copy.wait()


def row_sums(value):
    peak = jnp.max(value, axis=1, keepdims=True)
    total = jnp.sum(jnp.exp(value - peak), axis=1, keepdims=True)
    return jnp.broadcast_to(peak, (32, 128)), jnp.broadcast_to(total, (32, 128))


def early_body(scale, *refs):
    data, norms, noise = refs[0:2], refs[2], refs[3:7]
    terms, nn, scores, peaks, totals = refs[7:12]
    high, low, sems = refs[12:]
    copies = []
    for k in range(3):
        rows = slice(256 * k, 256 * k + 256)
        for i, (source, target) in enumerate(zip(data, (high, low))):
            copies.append(
                pltpu.make_async_copy(source.at[rows, :], target.at[rows, :], sems.at[2 * k + i])
            )
            copies[-1].start()
    middle = noise[0].shape[1]
    for p in range(16):
        q = second(p)
        one = noise[p // 8][32 * (p % 8) : 32 * (p % 8) + 32, :]
        two = noise[2 + q // 8][32 * (q % 8) : 32 * (q % 8) + 32, :]
        top, under = slice(32 * p, 32 * p + 32), slice(ROWS + 32 * p, ROWS + 32 * p + 32)
        terms[top, :middle], terms[under, :middle] = split(one)
        terms[top, middle:], terms[under, middle:] = split(two)
        total = jnp.sum(one * one + two * two, axis=1, keepdims=True)
        nn[32 * p : 32 * p + 32, :] = jnp.broadcast_to(total, (32, 128))
    for copy in copies:
        copy.wait()
    for half in range(2):
        for k in range(3):
            rows = slice(256 * k, 256 * k + 256)
            score(k, scale, terms, nn, high, low, norms.at[rows, :], scores, rows, half)
        for p in range(8 * half, 8 * half + 8):
            peaks[block(p), :], totals[block(p), :] = row_sums(scores[block(p), :])


def late_body(scale, places, own, sibling, terms, nn, peaks, totals, scores, out, dh, dl, *scratch):
    high, low, norm, ends, sums, sems = scratch
    group(0, (own, sibling), high, low, norm)
    sent = [
        pltpu.make_async_copy(source, target, sems.at[i])
        for i, (source, target) in enumerate(((high, dh), (low, dl)))
    ]
    for copy in sent:
        copy.start()
    for half in range(2):
        score(0, scale, terms, nn, high, low, norm, scores, slice(0, 256), half)
        for p in range(8 * half, 8 * half + 8):
            peak, total = row_sums(scores[block(p), :])
            before = peaks[block(p), :]
            top = jnp.maximum(peak, before)
            ends[place(places, p), :] = top
            sums[place(places, p), :] = total * jnp.exp(peak - top) + totals[block(p), :] * jnp.exp(
                before - top
            )
    value = jnp.concatenate([compact(ends), compact(sums)], axis=0)
    for to in range(16):
        out[to] = value
    for copy in sent:
        copy.wait()


def col_first_body(rplaces, cplaces, got, early, late, plan, out, pots, ends):
    peak = got[0, 0:4, :]
    for one in range(1, 16):
        peak = jnp.maximum(peak, got[one, 0:4, :])
    total = got[0, 4:8, :] * jnp.exp(got[0, 0:4, :] - peak)
    for one in range(1, 16):
        total = total + got[one, 4:8, :] * jnp.exp(got[one, 0:4, :] - peak)
    spread(math.log(DATA) - (peak + jnp.log(total)), pots)
    for k in range(4):
        lanes = slice(256 * k, 256 * k + 256)
        high = None
        for p in range(16):
            value = late[block(p), :] if k == 3 else early[block(p), lanes]
            value = value + pots[place(rplaces, p), :][:, :1]
            plan[block(p), lanes] = value
            value = jnp.max(value.reshape(4, 8, 256), axis=0)
            high = value if high is None else jnp.maximum(high, value)
        high = jnp.max(high, axis=0, keepdims=True)
        sums = None
        for p in range(16):
            value = jnp.exp(plan[block(p), lanes] - high)
            plan[block(p), lanes] = value
            value = jnp.sum(value.reshape(4, 8, 256), axis=0)
            sums = value if sums is None else sums + value
        sums = jnp.sum(sums, axis=0, keepdims=True)
        for half in range(2):
            at = cplaces[2 * k + half]
            ends[pl.ds(at, 1), :] = high[:, 128 * half : 128 * half + 128]
            ends[pl.ds(8 + at, 1), :] = sums[:, 128 * half : 128 * half + 128]
    for to in range(8):
        out[to] = ends[...]


def to_lanes(cplaces, ref):
    return jnp.concatenate([ref[pl.ds(cplaces[b], 1), :] for b in range(8)], axis=1)


def row_second_body(rplaces, cplaces, got, plan, out, gains, totals):
    high = got[0, 0:8, :]
    for one in range(1, 8):
        high = jnp.maximum(high, got[one, 0:8, :])
    total = got[0, 8:16, :] * jnp.exp(got[0, 0:8, :] - high)
    for one in range(1, 8):
        total = total + got[one, 8:16, :] * jnp.exp(got[one, 0:8, :] - high)
    own = got[pl.ds(cplaces[8], 1)][0, 0:8, :]
    gains[...] = NOISE * jnp.exp(own - high) / total
    lanes = to_lanes(cplaces, gains)
    for p in range(16):
        value = jnp.sum(plan[block(p), :] * lanes, axis=1, keepdims=True)
        totals[place(rplaces, p), :] = jnp.broadcast_to(value, (32, 128))
    value = compact(totals)
    value = jnp.concatenate([value, value], axis=0)
    for to in range(16):
        out[to] = value


def col_second_body(rplaces, cplaces, got, gains, plan, out, scales, ends):
    total = got[0, 0:4, :]
    for one in range(1, 16):
        total = total + got[one, 0:4, :]
    spread(DATA / total, scales)
    sums = None
    for p in range(16):
        value = plan[block(p), :] * scales[place(rplaces, p), :][:, :1]
        value = jnp.sum(value.reshape(4, 8, COLS), axis=0)
        sums = value if sums is None else sums + value
    sums = jnp.sum(sums, axis=0, keepdims=True)
    for b in range(8):
        ends[pl.ds(cplaces[b], 1), :] = sums[:, 128 * b : 128 * b + 128]
    value = ends[...] * gains[...]
    for to in range(8):
        out[to] = value


def weight_body(cplaces, got, gains, plan, high, low, denom, ends, totals):
    total = got[0]
    for one in range(1, 8):
        total = total + got[one]
    ends[...] = gains[...] * (NOISE / total)
    lanes = to_lanes(cplaces, ends)
    for p in range(16):
        value = plan[block(p), :] * lanes
        high[block(p), :], low[block(p), :] = split(value)
        totals[block(p), :] = jnp.broadcast_to(jnp.sum(value, axis=1, keepdims=True), (32, 128))
    denom[...] = totals[...]


def dot(one, two):
    return jnp.dot(one, two, preferred_element_type=F32)


def product_body(blocks, chunks, wh, wl, denom, h0, l0, h1, l1, *outs):
    terms = [
        jnp.concatenate([ref[block(p), at] for ref in (wh, wl) for p in blocks], axis=0)
        for at in (slice(0, 768), slice(768, 1024))
    ]
    for chunk, out in zip(chunks, outs):
        for n in range(2):
            at = slice(512 * chunk + 256 * n, 512 * chunk + 256 * n + 256)
            both = dot(terms[0], h0[:, at]) + dot(terms[1], h1[:, at])
            more = dot(terms[0][:256], l0[:, at]) + dot(terms[1][:256], l1[:, at])
            total = both[:256] + both[256:] + more
            for i in range(8):
                for t in range(2):
                    tile = total[32 * i : 32 * i + 32, 128 * t : 128 * t + 128]
                    out[i, 32 * (2 * n + t) : 32 * (2 * n + t) + 32, :] = tile
        if chunk == 0:
            eye = diagonal()[:32, :]
            for i, p in enumerate(blocks):
                row = jnp.sum(jnp.where(eye, denom[block(p), :], 0.0), axis=0, keepdims=True)
                out[i, 128:136, :] = jnp.broadcast_to(row, (8, 128))


def end_body(one, two, three, four, noise, times, path, velocity):
    eye = diagonal()[:32, :]

    def total(rows):
        return (one[rows, :] + two[rows, :]) + (three[rows, :] + four[rows, :])

    wide = jnp.broadcast_to(total(slice(128, 136))[:1, :], (32, 128))
    inverse = 1.0 / jnp.sum(jnp.where(eye, wide, 0.0), axis=1, keepdims=True)
    for t in range(16):
        lanes = slice(128 * t, 128 * t + 128)
        first = 32 * t + (0 if t < 4 else 8)
        target = total(slice(first, first + 32)) * inverse
        own = noise[:, lanes]
        at = times[:, :1]
        path[:, lanes] = (1.0 - at) * own + at * target
        velocity[:, lanes] = target - own


def after(*values):
    return lax.optimization_barrier(values)


def product(blocks, chunks, *arrays):
    return call(
        lambda *refs: product_body(blocks, chunks, *refs),
        tuple(shape((8, 136 if chunk == 0 else 128, 128)) for chunk in chunks),
        0,
        7,
    )(*arrays)


ORDER_1 = list(range(16))
ORDER_2 = [second(p) for p in ORDER_1]


def per_device(noise, data, times):
    features = noise.shape[1]
    middle = features // 2
    scale = 1.0 / (features * EPS)
    rplaces, cplaces = row_places(), col_places()

    near, far = swap_z(data, ZA), swap_z(data, ZB)
    parts = [noise[:, :middle], noise[:, middle:]]
    orders = (FIRST, SECOND)
    stages = []
    for step in range(3):
        parts = [
            jnp.concatenate([part, swap_col(part, order[step])], axis=0)
            for part, order in zip(parts, orders)
        ]
        stages.append(parts)
    last = [swap_col(part, order[3]) for part, order in zip(parts, orders)]
    first = data
    near = after(near, *stages[1])[0]
    own = [data, near, far, swap_z(near, ZB)]
    cross = [swap_core(first), swap_core(near), swap_core(far), swap_core(own[3])]
    pieces = [[part, one] for part, one in zip(parts, last)]

    wide = pltpu.VMEM((ROWS, 128), F32)
    norms, h0, l0 = call(
        data_body,
        (shape((768, 128)),) + (shape((768, features), BF),) * 2,
        scratch=(
            pltpu.VMEM((6, 128, features), F32),
            pltpu.VMEM((768, features), BF),
            pltpu.VMEM((768, features), BF),
            pltpu.SemaphoreType.DMA((6,)),
            pltpu.SemaphoreType.DMA((6,)),
        ),
        moved=12 * 2**20,
        far=6,
        far_out=2,
    )(own[0], cross[0], own[1], cross[1], own[2], cross[2])
    rows, row_norms, early, peaks, totals = call(
        lambda *refs: early_body(scale, *refs),
        (shape((2 * ROWS, features), BF), shape((ROWS, 128)), shape((ROWS, 768)))
        + (shape((ROWS, 128)),) * 2,
        arrays=5,
        scratch=(
            pltpu.VMEM((768, features), BF),
            pltpu.VMEM((768, features), BF),
            pltpu.SemaphoreType.DMA((6,)),
        ),
        flops=3 * 2 * ROWS * 768 * features,
        moved=16 * 2**20,
        limit=20,
        far=2,
    )(h0, l0, norms, *pieces[0], *pieces[1])
    late, send, h1, l1 = call(
        lambda *refs: late_body(scale, *refs),
        (shape((ROWS, 256)), shape((16, 8, 128))) + (shape((256, features), BF),) * 2,
        1,
        6,
        scratch=(
            pltpu.VMEM((256, features), BF),
            pltpu.VMEM((256, features), BF),
            pltpu.VMEM((256, 128), F32),
            wide,
            wide,
            pltpu.SemaphoreType.DMA((2,)),
        ),
        flops=3 * 2 * ROWS * 256 * features,
        moved=8 * 2**20,
        far_out=2,
    )(rplaces, own[3], cross[3], rows, row_norms, peaks, totals)
    send, rplaces, cplaces = after(send, rplaces, cplaces)
    got = lax.all_to_all(send, "col", 0, 0)
    plan, send = call(
        col_first_body,
        (shape((ROWS, COLS)), shape((8, 16, 128))),
        2,
        3,
        (wide, pltpu.VMEM((16, 128), F32)),
    )(rplaces, cplaces, got, early, late)
    got = lax.all_to_all(send, "row", 0, 0)
    send, gains = call(
        row_second_body,
        (shape((16, 8, 128)), shape((8, 128))),
        2,
        2,
        (wide,),
    )(rplaces, cplaces, got, plan)
    got = lax.all_to_all(send, "col", 0, 0)
    send = call(
        col_second_body,
        shape((8, 8, 128)),
        2,
        3,
        (wide, pltpu.VMEM((8, 128), F32)),
    )(rplaces, cplaces, got, gains, plan)
    got = lax.all_to_all(send, "row", 0, 0)
    wh, wl, denom = call(
        weight_body,
        (shape((ROWS, COLS), BF), shape((ROWS, COLS), BF), shape((ROWS, 128))),
        1,
        3,
        (pltpu.VMEM((8, 128), F32), wide),
    )(cplaces, got, gains, plan)

    rest = (wh, wl, denom, h0, l0, h1, l1)
    halves = ((ORDER_1, (0, 1), FIRST[::-1]), (ORDER_2, (2, 3), SECOND[::-1]))
    leaving = {}
    for i in range(2):
        for blocks, chunks, steps in halves:
            (out,) = product(blocks[8:], (chunks[i],), *rest)
            out, *rest = after(out, *rest)
            leaving[chunks[i]] = swap_col(out, steps[0])
    sums = {}
    for blocks, chunks, steps in halves:
        out = product(blocks[:8], chunks, *rest)
        *out, denom = after(*out, rest[2])
        rest = (rest[0], rest[1], denom) + tuple(rest[3:])
        sums.update(zip(chunks, out))
    order = [(chunks[i], steps) for i in range(2) for _, chunks, steps in halves]
    last = rest[2]
    for chunk, steps in order:
        sums[chunk] = last = sums[chunk] + after(leaving[chunk], last)[0]
        leaving[chunk] = swap_col(last[4:], steps[1])
    for chunk, steps in order:
        sums[chunk] = last = sums[chunk][:4] + after(leaving[chunk], last)[0]
    places = {(0, 0): (0, 0), VA: (1, 2), VB: (2, 1), VC: (3, 3)}

    def piece(masks):
        at = places[masks]
        return jnp.concatenate([sums[chunk][at[chunk // 2]] for chunk in range(4)], axis=0)

    parts = [piece((0, 0))] + [swap_col(piece(masks), masks) for masks in (VC, VA, VB)]
    wide_times = jnp.broadcast_to(times[:, None], (times.shape[0], 128))
    outs = (shape(noise.shape), shape(noise.shape))
    return call(end_body, outs, 0, 6)(*parts, noise, wide_times)


def solution(mesh):
    in_specs = (P(("row", "col"), None), P(("col", "row"), None), P(("row", "col")))
    out_specs = (P(("row", "col"), None), P(("row", "col"), None))
    return jax.shard_map(
        per_device, mesh=mesh, in_specs=in_specs, out_specs=out_specs, check_vma=False
    )
```
